128 devices in a mesh: gx: 4 (over z_hi, core), gy: 8 (over z_lo, y), gz: 4 (over x).
Axes of the slice: x: 4, y: 4, z: 4 (z_hi: 2, z_lo: 2; z = z_hi * 2 + z_lo), core: 2. Of those that a mesh axis runs over, the one named last changes fastest.
Arguments:
- tokens: bfloat16 [1024, 6144], P('gx', ('gy', 'gz')), may hold values from -6 to 6
- weight_in: bfloat16 [6144, 24576], P('gy', ('gx', 'gz')), may hold values from -0.078125 to 0.078125
- weight_out: bfloat16 [24576, 6144], P(('gx', 'gz'), 'gy'), may hold values from -0.0390625 to 0.0390625
- grad_out: bfloat16 [1024, 6144], P('gx', ('gy', 'gz')), may hold values from -6 to 6
Outputs:
- out: bfloat16 [1024, 6144], P('gx', ('gy', 'gz'))
- grad_tokens: bfloat16 [1024, 6144], P('gx', ('gy', 'gz'))
- grad_weight_in: bfloat16 [6144, 24576], P('gy', ('gx', 'gz'))
- grad_weight_out: bfloat16 [24576, 6144], P(('gx', 'gz'), 'gy')
The draws below stay inside these ranges and needn't reach their ends.
All inputs are finite; a program needn't handle non-finite values.
Results may differ from the reference program's by a relative error of at most 0.025.
Values may be sent and summed in bfloat16 or wider, within the bound.
No kernel may reach another device: no remote copies, remote signals or barrier semaphores. Data moves between devices by JAX's collectives and lax.ppermute only.
A program may use at most 128 MiB of HBM per device.

```python
import jax
import jax.numpy as jnp
from jax import lax

D = 6144
FF = 24576
TOK_DEV = 256
TOKENS = 1024
KBLK = 768


def level_of(rng, shape, pieces, least, top_value):
    def one(axis_at, blocks):
        draws = jax.random.uniform(jax.random.fold_in(jax.random.fold_in(rng, 6), axis_at), (blocks,), jnp.float32, least / len(pieces), top_value / len(pieces))
        return jnp.repeat(jnp.exp(draws), shape[axis_at] // blocks).reshape((-1,) + (1,) * (len(shape) - axis_at - 1))

    loudness = one(*pieces[0])
    for cut in pieces[1:]:
        loudness = loudness * one(*cut)
    return loudness


def gaussian(stream_key, extent, deviation, limit, shards=(), dtype=jnp.bfloat16):
    level = level_of(stream_key, extent, shards, -0.22, 0.18) if shards else 1.0
    values = jax.random.normal(stream_key, extent, jnp.float32) * deviation * level
    return jnp.minimum(jnp.maximum(values, -limit), limit).astype(dtype)


def setup_inputs(seed: int = 0) -> dict:
    splits = jax.random.split(jax.random.key(seed), 5)
    tokens = gaussian(splits[0], (TOKENS, D), 1.0, 6.0, ((0, 4), (1, 32)))
    weight_in = gaussian(splits[1], (D, FF), D ** -0.5, 0.078125, ((0, 8), (1, 16)))
    weight_out = gaussian(splits[2], (FF, D), FF ** -0.5, 0.0390625, ((0, 16), (1, 8)))
    grad_out = gaussian(splits[3], (TOKENS, D), 1.0, 6.0, ((0, 4), (1, 32)))
    return {"tokens": tokens, "weight_in": weight_in, "weight_out": weight_out, "grad_out": grad_out}


half_root = 0.7071067811865476
inv_root_tau = 0.3989422804014327


def gelu_value(preact):
    return 0.5 * preact * (1.0 + jax.scipy.special.erf(preact * half_root))


def gelu_slope(preact):
    return 0.5 * (1.0 + jax.scipy.special.erf(preact * half_root)) + preact * inv_root_tau * jnp.exp(-0.5 * preact * preact)


def rounded(values):
    return lax.optimization_barrier(values.astype(jnp.bfloat16)).astype(jnp.float32)


def width_blocks(left, right_blocks):
    rows = left.shape[0]
    count = right_blocks.shape[0]
    left_blocks = left.reshape(rows, count, KBLK).transpose(1, 0, 2)

    def accumulate(total, paired):
        return total + rounded(jnp.dot(paired[0], paired[1], preferred_element_type=jnp.float32)), None

    start = jnp.zeros((rows, right_blocks.shape[2]), jnp.float32)
    total, unused = lax.scan(accumulate, start, (left_blocks, right_blocks))
    return total


def token_blocks(left, right):
    count = left.shape[0] // TOK_DEV
    left_blocks = left.reshape(count, TOK_DEV, left.shape[1])
    right_blocks = right.reshape(count, TOK_DEV, right.shape[1])

    def accumulate(total, paired):
        product = lax.dot_general(paired[0], paired[1], (((0,), (0,)), ((), ())), preferred_element_type=jnp.float32)
        return total + rounded(product), None

    start = jnp.zeros((left.shape[1], right.shape[1]), jnp.float32)
    total, unused = lax.scan(accumulate, start, (left_blocks, right_blocks))
    return total


def reference(tokens, weight_in, weight_out, grad_out):
    count = D // KBLK
    preact = width_blocks(tokens, weight_in.reshape(count, KBLK, FF))
    active = gelu_value(preact).astype(jnp.bfloat16)
    out = jnp.dot(active, weight_out, preferred_element_type=jnp.float32).astype(jnp.bfloat16)
    grad_active = width_blocks(grad_out, weight_out.reshape(FF, count, KBLK).transpose(1, 2, 0))
    grad_preact = (grad_active * gelu_slope(preact)).astype(jnp.bfloat16)
    grad_weight_out = token_blocks(active, grad_out).astype(jnp.bfloat16)
    grad_weight_in = token_blocks(tokens, grad_preact).astype(jnp.bfloat16)
    grad_tokens = lax.dot_general(grad_preact, weight_in, (((1,), (1,)), ((), ())), preferred_element_type=jnp.float32).astype(jnp.bfloat16)
    return out, grad_tokens, grad_weight_in, grad_weight_out
```

```python
import jax
import jax.numpy as jnp
from jax import lax
from jax.sharding import PartitionSpec as P

half_root = 0.7071067811865476
inv_root_tau = 0.3989422804014327
bf16 = jnp.bfloat16
f32 = jnp.float32


def gelu_value(preact):
    return 0.5 * preact * (1.0 + jax.scipy.special.erf(preact * half_root))


def gelu_slope(preact):
    return 0.5 * (
        1.0 + jax.scipy.special.erf(preact * half_root)
    ) + preact * inv_root_tau * jnp.exp(-0.5 * preact * preact)


def dot_nn(left, right):
    return lax.dot_general(left, right, (((1,), (0,)), ((), ())), preferred_element_type=f32)


def dot_tn(left, right):
    return lax.dot_general(left, right, (((0,), (0,)), ((), ())), preferred_element_type=f32)


def dot_nt(left, right):
    return lax.dot_general(left, right, (((1,), (1,)), ((), ())), preferred_element_type=f32)


def corner(place):
    return place ^ (place >> 1)


GY_PAIRS = {
    2: [(g, g ^ 4) for g in range(8)],
    1: [(g, (g & 4) | (3 - (g & 3))) for g in range(8)],
    0: [(g, g ^ 1) for g in range(8)],
}
GZ_PAIRS = {
    1: [(g, 3 - g) for g in range(4)],
    0: [(g, g ^ 1) for g in range(4)],
}
CORE_PAIRS = [(g, g ^ 1) for g in range(4)]
HIGH_PAIRS = [(g, g ^ 2) for g in range(4)]

PARTS = 3
ORDERS = ((2, 1, 0), (1, 0, 2), (0, 2, 1))


def over_gy(block, bit):
    return lax.ppermute(block, "gy", GY_PAIRS[bit])


def over_gz(block, bit):
    return lax.ppermute(block, "gz", GZ_PAIRS[bit])


def pick(array, axis, index):
    return lax.index_in_dim(array, index, axis, keepdims=False)


def permute_leading(blocks, ident, count):
    return [lax.dynamic_index_in_dim(blocks, p ^ ident, 0, keepdims=False) for p in range(count)]


def per_device(tokens, weight_in, weight_out, grad_out):
    gy = lax.axis_index("gy")
    gy_id = (gy & 4) | corner(gy & 3)
    gz_id = corner(lax.axis_index("gz"))
    rows = tokens.shape[0] // 8
    width = tokens.shape[1]
    hidden = weight_in.shape[1]
    part = hidden // PARTS

    def gather(shard):
        own = jnp.stack(permute_leading(shard.reshape(8, rows, width), gy_id, 8))
        other = lax.ppermute(own, "gx", HIGH_PAIRS)
        spread = []
        for half, order in ((own, (0, 1)), (other, (1, 0))):
            first = over_gz(half, order[0])
            pair = jnp.stack([half, first])
            second = over_gz(pair, order[1])
            square = jnp.stack([pair, second])
            if order == (1, 0):
                square = jnp.swapaxes(square, 0, 1)
            square = square.reshape(4, 8, rows, width)
            spread.append(
                jnp.concatenate(
                    [lax.dynamic_index_in_dim(square, corner(p) ^ gz_id, 0, False) for p in range(4)], axis=-1
                )
            )
        mine = jnp.stack(spread, axis=1)
        theirs = lax.ppermute(mine, "gx", CORE_PAIRS)
        full = jnp.stack([mine, theirs], axis=1)
        return full.reshape(2, 2, 2, 2, 2, rows, 4 * width)

    def scatter_out(terms_of):
        theirs = lax.ppermute(terms_of(1).astype(bf16), "gx", CORE_PAIRS)
        mine = (terms_of(0) + theirs.astype(f32)).astype(bf16)
        mine = mine.reshape(8, 2, rows, 4, width)
        done = []
        for high, order in ((0, (0, 1)), (1, (1, 0))):
            half = mine[:, high].transpose(2, 0, 1, 3)
            half = [lax.dynamic_index_in_dim(half, corner(p ^ gz_id), 0, False) for p in range(4)]
            half = jnp.stack(half).reshape(2, 2, 8 * rows, width)
            axis = 1 - order[0]
            got = over_gz(pick(half, axis, 1), order[0])
            half = (pick(half, axis, 0).astype(f32) + got.astype(f32)).astype(bf16)
            got = over_gz(half[1], order[1])
            done.append((half[0].astype(f32) + got.astype(f32)).astype(bf16))
        got = lax.ppermute(done[1], "gx", HIGH_PAIRS)
        total = (done[0].astype(f32) + got.astype(f32)).astype(bf16)
        total = permute_leading(total.reshape(8, rows, width), gy_id, 8)
        return jnp.concatenate(total, axis=0)

    def reduce_gy(left, times, order):
        depth = left.shape[-1]
        first, second, third = order
        sent = pick(left, 2 - first, 1).reshape(-1, depth)
        got = over_gy(times(sent).astype(bf16), first)
        held = times(pick(left, 2 - first, 0).reshape(-1, depth)) + got.astype(f32)
        rest = [bit for bit in (2, 1, 0) if bit != first]
        held = held.reshape(2, 2, 4 * rows, part)
        axis = rest.index(second)
        got = over_gy(pick(held, axis, 1).astype(bf16), second)
        held = pick(held, axis, 0) + got.astype(f32)
        got = over_gy(held[1].astype(bf16), third)
        return held[0] + got.astype(f32)

    def gather_gy(piece, order):
        first, second, third = order
        pair = jnp.stack([piece, over_gy(piece, third)])
        square = jnp.stack([pair, over_gy(pair, second)])
        cube = jnp.stack([square, over_gy(square, first)])
        axes = [order.index(bit) for bit in (2, 1, 0)]
        cube = cube.transpose(*axes, 3, 4)
        return cube.reshape(2, 2, 2, 2, 2, rows, part)

    features = gather(tokens)
    grad_feats = gather(grad_out)

    actives, grads = [], []
    spans = [(i * part, (i + 1) * part) for i in range(PARTS)]
    for (lo, hi), order in zip(spans, ORDERS):
        preact = reduce_gy(features, lambda u: dot_nn(u, weight_in[:, lo:hi]), order)
        actives.append(gelu_value(preact).astype(bf16))
        grad_active = reduce_gy(grad_feats, lambda u: dot_nt(u, weight_out[lo:hi]), order)
        grads.append((grad_active * gelu_slope(preact)).astype(bf16))
    active_rows = jnp.concatenate([gather_gy(u, o) for u, o in zip(actives, ORDERS)], axis=-1)
    grad_rows = jnp.concatenate([gather_gy(u, o) for u, o in zip(grads, ORDERS)], axis=-1)

    out = scatter_out(lambda core: dot_nn(active_rows[:, :, :, core].reshape(-1, hidden), weight_out))
    grad_tokens = scatter_out(lambda core: dot_nt(grad_rows[:, :, :, core].reshape(-1, hidden), weight_in))
    grad_weight_out = dot_tn(
        active_rows.reshape(-1, hidden), grad_feats.reshape(-1, 4 * width)
    ).astype(bf16)
    grad_weight_in = dot_tn(
        features.reshape(-1, 4 * width), grad_rows.reshape(-1, hidden)
    ).astype(bf16)
    return (out, grad_tokens, grad_weight_in, grad_weight_out)


def solution(mesh):
    return jax.shard_map(
        per_device,
        mesh=mesh,
        in_specs=(
            P("gx", ("gy", "gz")),
            P("gy", ("gx", "gz")),
            P(("gx", "gz"), "gy"),
            P("gx", ("gy", "gz")),
        ),
        out_specs=(
            P("gx", ("gy", "gz")),
            P("gx", ("gy", "gz")),
            P("gy", ("gx", "gz")),
            P(("gx", "gz"), "gy"),
        ),
        check_vma=False,
    )
```

```python
import jax
import jax.numpy as jnp
from jax import lax
from jax.experimental import pallas as pl
from jax.experimental.pallas import tpu as pltpu
from jax.sharding import PartitionSpec as P

half_root = 0.7071067811865476
inv_root_tau = 0.3989422804014327
bf16 = jnp.bfloat16
f32 = jnp.float32


def gelu_value(preact):
    return 0.5 * preact * (1.0 + jax.scipy.special.erf(preact * half_root))


def gelu_slope(preact):
    return 0.5 * (
        1.0 + jax.scipy.special.erf(preact * half_root)
    ) + preact * inv_root_tau * jnp.exp(-0.5 * preact * preact)


def dot_nn(left, right):
    return lax.dot_general(left, right, (((1,), (0,)), ((), ())), preferred_element_type=f32)


def dot_tn(left, right):
    return lax.dot_general(left, right, (((0,), (0,)), ((), ())), preferred_element_type=f32)


def dot_nt(left, right):
    return lax.dot_general(left, right, (((1,), (1,)), ((), ())), preferred_element_type=f32)


def corner(place):
    return place ^ (place >> 1)


GY_PAIRS = {
    2: [(g, g ^ 4) for g in range(8)],
    1: [(g, (g & 4) | (3 - (g & 3))) for g in range(8)],
    0: [(g, g ^ 1) for g in range(8)],
}
GZ_PAIRS = {step: [(g, corner(corner(g) ^ step)) for g in range(4)] for step in (1, 2, 3)}
CORE_PAIRS = [(g, g ^ 1) for g in range(4)]
HIGH_PAIRS = [(g, g ^ 2) for g in range(4)]

PARTS = 3
ORDERS = ((2, 1, 0), (1, 0, 2), (0, 2, 1))
SLOT = 256


def over_gy(block, bit):
    return lax.ppermute(block, "gy", GY_PAIRS[bit])


def over_gz(block, step):
    return lax.ppermute(block, "gz", GZ_PAIRS[step])


def over_core(block):
    return lax.ppermute(block, "gx", CORE_PAIRS)


def over_high(block):
    return lax.ppermute(block, "gx", HIGH_PAIRS)


def pick(array, axis, index):
    return lax.index_in_dim(array, index, axis, keepdims=False)


def dyn(array, index):
    return lax.dynamic_index_in_dim(array, index, 0, keepdims=False)


def pass_on(*refs):
    pass


def gate(values, last):
    values, last = tuple(values), tuple(last)
    anywhere = pl.BlockSpec(memory_space=pl.ANY)
    return pl.pallas_call(
        pass_on,
        out_shape=[jax.ShapeDtypeStruct(v.shape, v.dtype) for v in values],
        in_specs=[anywhere] * (len(values) + len(last)),
        out_specs=[anywhere] * len(values),
        input_output_aliases={i: i for i in range(len(values))},
        compiler_params=pltpu.CompilerParams(vmem_limit_bytes=1 << 20),
    )(*values, *last)


def per_device(tokens, weight_in, weight_out, grad_out):
    gy = lax.axis_index("gy")
    gy_id = (gy & 4) | corner(gy & 3)
    gz_id = corner(lax.axis_index("gz"))
    rows = tokens.shape[0] // 8
    width = tokens.shape[1]
    hidden = weight_in.shape[1]
    part = hidden // PARTS
    slot = max(SLOT, width)
    depth = 4 * width

    both = jnp.concatenate([tokens, grad_out], axis=1).reshape(8, rows, 2 * width)
    own = jnp.stack([dyn(both, p ^ gy_id) for p in range(8)])
    squares = [jnp.stack([half] + [over_gz(half, step) for step in (1, 2, 3)]) for half in (own, over_high(own))]
    squares = [[dyn(square, corner(p) ^ gz_id) for p in range(4)] for square in squares]
    sides = []
    for lo in (0, width):
        spread = [jnp.concatenate([s[..., lo : lo + width] for s in square], axis=-1) for square in squares]
        mine = jnp.stack(spread, axis=1)
        sides.append(jnp.stack([mine, over_core(mine)], axis=1).reshape(2, 2, 2, 2, 2, rows, depth))
    features, grad_feats = sides

    def add(left, right):
        return left.astype(f32) + right.astype(f32)

    def reduce_gy(terms, order):
        first, second, third = order
        got = over_gy(pick(terms, 2 - first, 1), first)
        held = add(pick(terms, 2 - first, 0), got)
        axis = [bit for bit in (2, 1, 0) if bit != first].index(second)
        got = over_gy(pick(held, axis, 1).astype(bf16), second)
        held = pick(held, axis, 0) + got.astype(f32)
        got = over_gy(held[1].astype(bf16), third)
        return held[0] + got.astype(f32)

    def gather_gy(piece, order):
        first, second, third = order
        pair = jnp.stack([piece, over_gy(piece, third)])
        square = jnp.stack([pair, over_gy(pair, second)])
        cube = jnp.stack([square, over_gy(square, first)])
        axes = [order.index(bit) for bit in (2, 1, 0)]
        return cube.transpose(*axes, 3, 4).reshape(2, 2, 2, 2, 2, rows, part)

    actives, grads = [], []
    spans = [(i * part, (i + 1) * part) for i in range(PARTS)]
    terms = dot_nn(features.reshape(-1, depth), weight_in).astype(bf16).reshape(2, 2, 2, 4 * rows, hidden)
    grad_terms = dot_nt(grad_feats.reshape(-1, depth), weight_out).astype(bf16).reshape(2, 2, 2, 4 * rows, hidden)
    for (lo, hi), order in zip(spans, ORDERS):
        preact = reduce_gy(terms[..., lo:hi], order)
        actives.append(gelu_value(preact).astype(bf16))
        grad_active = reduce_gy(grad_terms[..., lo:hi], order)
        grads.append((grad_active * gelu_slope(preact)).astype(bf16))
    active_rows = jnp.concatenate([gather_gy(u, o) for u, o in zip(actives, ORDERS)], axis=-1)
    grad_rows = jnp.concatenate([gather_gy(u, o) for u, o in zip(grads, ORDERS)], axis=-1)

    gz_late = gz_id + (actives[0][0, 0].astype(f32) * 0.0).astype(jnp.int32)

    def slots(pieces, axis):
        full = []
        for p in range(4):
            place = corner(p ^ gz_late)
            low = jnp.where(place & 1 == 1, pieces[1], pieces[0])
            high = jnp.where(place & 1 == 1, pieces[3], pieces[2])
            piece = jnp.where(place >= 2, high, low)
            wide = [(0, 0), (0, 0)]
            wide[axis] = (0, slot - width)
            full.append(jnp.pad(piece, wide))
        return jnp.concatenate(full, axis=axis)

    slots_out = slots([weight_out[:, p * width : (p + 1) * width] for p in range(4)], 1)
    slots_in = slots([weight_in[p * width : (p + 1) * width] for p in range(4)], 0)

    def core_sum(times, full):
        away = times(full[:, :, :, 1].reshape(-1, hidden)).astype(bf16)
        return add(times(full[:, :, :, 0].reshape(-1, hidden)), over_core(away)).astype(bf16)

    def width_sum(mine):
        got = [over_gz(mine[:, step * slot : (step + 1) * slot], step) for step in (1, 2, 3)]
        total = mine[:, :slot].astype(f32)
        for block in got:
            total += block.astype(f32)
        return total.reshape(8, 2, rows, slot), got[0]

    def high_sum(total):
        total = add(total[:, 0], over_high(total[:, 1].astype(bf16))).astype(bf16)[:, :, :width]
        return jnp.concatenate([dyn(total, p ^ gy_id) for p in range(8)], axis=0)

    out_mine = core_sum(lambda u: dot_nn(u, slots_out), active_rows)
    grad_mine = core_sum(lambda u: dot_nt(u, slots_in), grad_rows)
    out_total, out_first = width_sum(out_mine)
    grad_total, grad_first = width_sum(grad_mine)
    (grad_feats,) = gate([grad_feats], [out_first])
    (features,) = gate([features], [grad_first])
    grad_weight_out = dot_tn(active_rows.reshape(-1, hidden), grad_feats.reshape(-1, depth)).astype(bf16)
    grad_weight_in = dot_tn(features.reshape(-1, depth), grad_rows.reshape(-1, hidden)).astype(bf16)
    return (high_sum(out_total), high_sum(grad_total), grad_weight_in, grad_weight_out)


def solution(mesh):
    return jax.shard_map(
        per_device,
        mesh=mesh,
        in_specs=(
            P("gx", ("gy", "gz")),
            P("gy", ("gx", "gz")),
            P(("gx", "gz"), "gy"),
            P("gx", ("gy", "gz")),
        ),
        out_specs=(
            P("gx", ("gy", "gz")),
            P("gx", ("gy", "gz")),
            P("gy", ("gx", "gz")),
            P(("gx", "gz"), "gy"),
        ),
        check_vma=False,
    )
```

```python
import jax
import jax.numpy as jnp
from jax import lax
from jax.experimental import pallas as pl
from jax.experimental.pallas import tpu as pltpu
from jax.sharding import PartitionSpec as P

half_root = 0.7071067811865476
inv_root_tau = 0.3989422804014327
bf16 = jnp.bfloat16
f32 = jnp.float32


def gelu_value(preact):
    return 0.5 * preact * (1.0 + jax.scipy.special.erf(preact * half_root))


def gelu_slope(preact):
    return 0.5 * (
        1.0 + jax.scipy.special.erf(preact * half_root)
    ) + preact * inv_root_tau * jnp.exp(-0.5 * preact * preact)


def dot_nn(left, right):
    return lax.dot_general(left, right, (((1,), (0,)), ((), ())), preferred_element_type=f32)


def dot_tn(left, right):
    return lax.dot_general(left, right, (((0,), (0,)), ((), ())), preferred_element_type=f32)


def dot_nt(left, right):
    return lax.dot_general(left, right, (((1,), (1,)), ((), ())), preferred_element_type=f32)


def corner(place):
    return place ^ (place >> 1)


GY_PAIRS = {
    2: [(g, g ^ 4) for g in range(8)],
    1: [(g, (g & 4) | (3 - (g & 3))) for g in range(8)],
    0: [(g, g ^ 1) for g in range(8)],
}
GZ_PAIRS = {step: [(g, corner(corner(g) ^ step)) for g in range(4)] for step in (1, 2, 3)}
CORE_PAIRS = [(g, g ^ 1) for g in range(4)]
HIGH_PAIRS = [(g, g ^ 2) for g in range(4)]

PARTS = 3
ORDERS = ((2, 1, 0), (1, 0, 2), (0, 2, 1))
SLOT = 256


def over_gy(block, bit):
    return lax.ppermute(block, "gy", GY_PAIRS[bit])


def over_gz(block, step):
    return lax.ppermute(block, "gz", GZ_PAIRS[step])


def over_core(block):
    return lax.ppermute(block, "gx", CORE_PAIRS)


def over_high(block):
    return lax.ppermute(block, "gx", HIGH_PAIRS)


def pick(array, axis, index):
    return lax.index_in_dim(array, index, axis, keepdims=False)


def dyn(array, index):
    return lax.dynamic_index_in_dim(array, index, 0, keepdims=False)


def pass_on(*refs):
    pass


def gate(values, last):
    values, last = tuple(values), tuple(last)
    anywhere = pl.BlockSpec(memory_space=pl.ANY)
    return pl.pallas_call(
        pass_on,
        out_shape=[jax.ShapeDtypeStruct(v.shape, v.dtype) for v in values],
        in_specs=[anywhere] * (len(values) + len(last)),
        out_specs=[anywhere] * len(values),
        input_output_aliases={i: i for i in range(len(values))},
        compiler_params=pltpu.CompilerParams(vmem_limit_bytes=1 << 20),
    )(*values, *last)


def per_device(tokens, weight_in, weight_out, grad_out):
    gy = lax.axis_index("gy")
    gy_id = (gy & 4) | corner(gy & 3)
    gz_id = corner(lax.axis_index("gz"))
    rows = tokens.shape[0] // 8
    width = tokens.shape[1]
    hidden = weight_in.shape[1]
    part = hidden // PARTS
    slot = max(SLOT, width)
    depth = 4 * width

    both = jnp.concatenate([tokens, grad_out], axis=1).reshape(8, rows, 2 * width)
    own = jnp.stack([dyn(both, p ^ gy_id) for p in range(8)])
    squares = [jnp.stack([half] + [over_gz(half, step) for step in (1, 2, 3)]) for half in (own, over_high(own))]
    squares = [[dyn(square, corner(p) ^ gz_id) for p in range(4)] for square in squares]
    sides = []
    for lo in (0, width):
        spread = [jnp.concatenate([s[..., lo : lo + width] for s in square], axis=-1) for square in squares]
        mine = jnp.stack(spread, axis=1)
        sides.append(jnp.stack([mine, over_core(mine)], axis=1).reshape(2, 2, 2, 2, 2, rows, depth))
    features, grad_feats = sides

    def add(left, right):
        return left.astype(f32) + right.astype(f32)

    spans = [(i * part, (i + 1) * part) for i in range(PARTS)]
    terms = dot_nn(features.reshape(-1, depth), weight_in).astype(bf16).reshape(2, 2, 2, 4 * rows, hidden)
    grad_terms = dot_nt(grad_feats.reshape(-1, depth), weight_out).astype(bf16).reshape(2, 2, 2, 4 * rows, hidden)
    cubes = ([], [])
    for (lo, hi), (first, second, third) in zip(spans, ORDERS):
        axis = 1 + [bit for bit in (2, 1, 0) if bit != first].index(second)
        away, held = (
            jnp.stack([pick(side[..., lo:hi], 2 - first, k) for side in (terms, grad_terms)]) for k in (1, 0)
        )
        held = add(held, over_gy(away, first)).astype(bf16)
        held = add(pick(held, axis, 0), over_gy(pick(held, axis, 1), second)).astype(bf16)
        if not cubes[0]:
            begun = held
        total = add(held[:, 0], over_gy(held[:, 1], third))
        active = gelu_value(total[0]).astype(bf16)
        grad = (total[1] * gelu_slope(total[0])).astype(bf16)
        piece = jnp.stack([active, grad])
        pair = jnp.stack([piece, over_gy(piece, third)], axis=1)
        square = jnp.stack([pair, over_gy(pair, second)], axis=1)
        axes = [(first, second, third).index(bit) for bit in (2, 1, 0)]
        for side, full in zip(square, cubes):
            cube = jnp.stack([side, over_gy(side, first)])
            full.append(cube.transpose(*axes, 3, 4).reshape(2, 2, 2, 2, 2, rows, part))
    active_rows, grad_rows = (jnp.concatenate(full, axis=-1) for full in cubes)

    gz_late = gz_id + (begun[0, 0, 0, 0].astype(f32) * 0.0).astype(jnp.int32)

    def slots(pieces, axis, fill):
        full = []
        for p in range(4):
            place = corner(p ^ gz_late)
            low = jnp.where(place & 1 == 1, pieces[1], pieces[0])
            high = jnp.where(place & 1 == 1, pieces[3], pieces[2])
            piece = jnp.where(place >= 2, high, low)
            wide = [(0, 0), (0, 0)]
            wide[axis] = fill
            full.append(jnp.pad(piece, wide))
        return jnp.concatenate(full, axis=axis)

    slots_out = slots([weight_out[:, p * width : (p + 1) * width] for p in range(4)], 1, (0, slot - width))
    slots_in = slots([weight_in[p * width : (p + 1) * width] for p in range(4)], 0, (slot - width, 0))

    def core_sum(times, full):
        away = times(full[:, :, :, 1].reshape(-1, hidden)).astype(bf16)
        return add(times(full[:, :, :, 0].reshape(-1, hidden)), over_core(away)).astype(bf16)

    out_mine = core_sum(lambda u: dot_nn(u, slots_out), active_rows)
    grad_mine = core_sum(lambda u: dot_nt(u, slots_in), grad_rows)
    lap = slot // 2

    def joined(p):
        left, right = (side[:, p * slot : (p + 1) * slot] for side in (out_mine, grad_mine))
        return jnp.concatenate([left[:, :lap], left[:, lap:] + right[:, :lap], right[:, lap:]], axis=1)

    got = [over_gz(joined(step), step) for step in (1, 2, 3)]
    features, grad_feats = gate([features, grad_feats], [out_mine, grad_mine])
    grad_weight_out = dot_tn(active_rows.reshape(-1, hidden), grad_feats.reshape(-1, depth)).astype(bf16)
    grad_weight_in = dot_tn(features.reshape(-1, depth), grad_rows.reshape(-1, hidden)).astype(bf16)
    total = joined(0).astype(f32)
    for block in gate(got, [grad_weight_out, grad_weight_in]):
        total += block.astype(f32)
    total = total.reshape(8, 2, rows, 3 * lap)
    total = add(total[:, 0], over_high(total[:, 1].astype(bf16))).astype(bf16)
    total = jnp.concatenate([dyn(total, p ^ gy_id) for p in range(8)], axis=0)
    return (total[:, :width], total[:, -width:], grad_weight_in, grad_weight_out)


def solution(mesh):
    return jax.shard_map(
        per_device,
        mesh=mesh,
        in_specs=(
            P("gx", ("gy", "gz")),
            P("gy", ("gx", "gz")),
            P(("gx", "gz"), "gy"),
            P("gx", ("gy", "gz")),
        ),
        out_specs=(
            P("gx", ("gy", "gz")),
            P("gx", ("gy", "gz")),
            P("gy", ("gx", "gz")),
            P(("gx", "gz"), "gy"),
        ),
        check_vma=False,
    )
```

```python
import jax
import jax.numpy as jnp
from jax import lax
from jax.experimental import pallas as pl
from jax.experimental.pallas import tpu as pltpu
from jax.sharding import PartitionSpec as P

half_root = 0.7071067811865476
inv_root_tau = 0.3989422804014327
bf16 = jnp.bfloat16
f32 = jnp.float32


def gelu_value(preact):
    return 0.5 * preact * (1.0 + jax.scipy.special.erf(preact * half_root))


def gelu_slope(preact):
    return 0.5 * (
        1.0 + jax.scipy.special.erf(preact * half_root)
    ) + preact * inv_root_tau * jnp.exp(-0.5 * preact * preact)


def dot_nn(left, right):
    return lax.dot_general(left, right, (((1,), (0,)), ((), ())), preferred_element_type=f32)


def dot_tn(left, right):
    return lax.dot_general(left, right, (((0,), (0,)), ((), ())), preferred_element_type=f32)


def dot_nt(left, right):
    return lax.dot_general(left, right, (((1,), (1,)), ((), ())), preferred_element_type=f32)


def corner(place):
    return place ^ (place >> 1)


GY_PAIRS = {
    2: [(g, g ^ 4) for g in range(8)],
    1: [(g, (g & 4) | (3 - (g & 3))) for g in range(8)],
    0: [(g, g ^ 1) for g in range(8)],
}
GZ_PAIRS = {step: [(g, corner(corner(g) ^ step)) for g in range(4)] for step in (1, 2, 3)}
CORE_PAIRS = [(g, g ^ 1) for g in range(4)]
HIGH_PAIRS = [(g, g ^ 2) for g in range(4)]

PARTS = 3
ORDERS = ((2, 1, 0), (1, 0, 2), (0, 2, 1))
SLOT = 256


def over_gy(block, bit):
    return lax.ppermute(block, "gy", GY_PAIRS[bit])


def over_gz(block, step):
    return lax.ppermute(block, "gz", GZ_PAIRS[step])


def over_core(block):
    return lax.ppermute(block, "gx", CORE_PAIRS)


def over_high(block):
    return lax.ppermute(block, "gx", HIGH_PAIRS)


def pick(array, axis, index):
    return lax.index_in_dim(array, index, axis, keepdims=False)


def dyn(array, index):
    return lax.dynamic_index_in_dim(array, index, 0, keepdims=False)


def pass_on(*refs):
    pass


def gate(values, last):
    values, last = tuple(values), tuple(last)
    anywhere = pl.BlockSpec(memory_space=pl.ANY)
    return pl.pallas_call(
        pass_on,
        out_shape=[jax.ShapeDtypeStruct(v.shape, v.dtype) for v in values],
        in_specs=[anywhere] * (len(values) + len(last)),
        out_specs=[anywhere] * len(values),
        input_output_aliases={i: i for i in range(len(values))},
        compiler_params=pltpu.CompilerParams(vmem_limit_bytes=1 << 20),
    )(*values, *last)


def per_device(tokens, weight_in, weight_out, grad_out):
    gy = lax.axis_index("gy")
    gy_id = (gy & 4) | corner(gy & 3)
    gz_id = corner(lax.axis_index("gz"))
    rows = tokens.shape[0] // 8
    width = tokens.shape[1]
    hidden = weight_in.shape[1]
    part = hidden // PARTS
    slot = max(SLOT, width)
    depth = 4 * width

    both = jnp.concatenate([tokens, grad_out], axis=1).reshape(8, rows, 2 * width)
    own = jnp.stack([dyn(both, p ^ gy_id) for p in range(8)])
    squares = [jnp.stack([half] + [over_gz(half, step) for step in (1, 2, 3)]) for half in (own, over_high(own))]
    squares = [[dyn(square, corner(p) ^ gz_id) for p in range(4)] for square in squares]
    sides = []
    for lo in (0, width):
        spread = [jnp.concatenate([s[..., lo : lo + width] for s in square], axis=-1) for square in squares]
        mine = jnp.stack(spread, axis=1)
        sides.append(jnp.stack([mine, over_core(mine)], axis=1).reshape(2, 2, 2, 2, 2, rows, depth))
    features, grad_feats = sides

    def add(left, right):
        return left.astype(f32) + right.astype(f32)

    spans = [(i * part, (i + 1) * part) for i in range(PARTS)]
    terms = dot_nn(features.reshape(-1, depth), weight_in).astype(bf16).reshape(2, 2, 2, 4 * rows, hidden)
    grad_terms = dot_nt(grad_feats.reshape(-1, depth), weight_out).astype(bf16).reshape(2, 2, 2, 4 * rows, hidden)
    cubes = ([], [])
    for (lo, hi), (first, second, third) in zip(spans, ORDERS):
        axis = 1 + [bit for bit in (2, 1, 0) if bit != first].index(second)
        away, held = (
            jnp.stack([pick(side[..., lo:hi], 2 - first, k) for side in (terms, grad_terms)]) for k in (1, 0)
        )
        held = add(held, over_gy(away, first)).astype(bf16)
        held = add(pick(held, axis, 0), over_gy(pick(held, axis, 1), second)).astype(bf16)
        total = add(held[:, 0], over_gy(held[:, 1], third))
        active = gelu_value(total[0]).astype(bf16)
        grad = (total[1] * gelu_slope(total[0])).astype(bf16)
        piece = jnp.stack([active, grad])
        pair = jnp.stack([piece, over_gy(piece, third)], axis=1)
        square = jnp.stack([pair, over_gy(pair, second)], axis=1)
        if not cubes[0]:
            begun = pair
        axes = [(first, second, third).index(bit) for bit in (2, 1, 0)]
        for side, full in zip(square, cubes):
            cube = jnp.stack([side, over_gy(side, first)])
            full.append(cube.transpose(*axes, 3, 4).reshape(2, 2, 2, 2, 2, rows, part))
    active_rows, grad_rows = (jnp.concatenate(full, axis=-1) for full in cubes)

    gz_late = gz_id + (begun[0, 0, 0, 0].astype(f32) * 0.0).astype(jnp.int32)

    def slots(pieces, axis, fill):
        full = []
        for p in range(4):
            place = corner(p ^ gz_late)
            low = jnp.where(place & 1 == 1, pieces[1], pieces[0])
            high = jnp.where(place & 1 == 1, pieces[3], pieces[2])
            piece = jnp.where(place >= 2, high, low)
            wide = [(0, 0), (0, 0)]
            wide[axis] = fill
            full.append(jnp.pad(piece, wide))
        return jnp.concatenate(full, axis=axis)

    slots_out = slots([weight_out[:, p * width : (p + 1) * width] for p in range(4)], 1, (0, slot - width))
    slots_in = slots([weight_in[p * width : (p + 1) * width] for p in range(4)], 0, (slot - width, 0))

    def core_sum(times, full):
        away = times(full[:, :, :, 1].reshape(-1, hidden)).astype(bf16)
        return add(times(full[:, :, :, 0].reshape(-1, hidden)), over_core(away)).astype(bf16)

    out_mine = core_sum(lambda u: dot_nn(u, slots_out), active_rows)
    grad_mine = core_sum(lambda u: dot_nt(u, slots_in), grad_rows)
    lap = slot // 2

    def joined(p):
        left, right = (side[:, p * slot : (p + 1) * slot] for side in (out_mine, grad_mine))
        return jnp.concatenate([left[:, :lap], left[:, lap:] + right[:, :lap], right[:, lap:]], axis=1)

    pieces = [joined(p).reshape(8, 2, rows, 3 * lap) for p in range(4)]
    orders = ((1, 2), (2, 1))
    got = [over_gz(jnp.stack([pieces[f][:, h], pieces[3][:, h]]), f) for h, (f, s) in enumerate(orders)]
    features, grad_feats = gate([features, grad_feats], [out_mine, grad_mine])
    grad_weight_out = dot_tn(active_rows.reshape(-1, hidden), grad_feats.reshape(-1, depth)).astype(bf16)
    grad_weight_in = dot_tn(features.reshape(-1, depth), grad_rows.reshape(-1, hidden)).astype(bf16)
    got = gate(got, [grad_weight_out])
    near = [
        add(jnp.stack([pieces[0][:, h], pieces[s][:, h]]), got[h]).astype(bf16) for h, (f, s) in enumerate(orders)
    ]
    got = gate([over_gz(near[h][1], s) for h, (f, s) in enumerate(orders)], [grad_weight_in])
    total = [add(side[0], block) for side, block in zip(near, got)]
    total = add(total[0], over_high(total[1].astype(bf16))).astype(bf16)
    total = jnp.concatenate([dyn(total, p ^ gy_id) for p in range(8)], axis=0)
    return (total[:, :width], total[:, -width:], grad_weight_in, grad_weight_out)


def solution(mesh):
    return jax.shard_map(
        per_device,
        mesh=mesh,
        in_specs=(
            P("gx", ("gy", "gz")),
            P("gy", ("gx", "gz")),
            P(("gx", "gz"), "gy"),
            P("gx", ("gy", "gz")),
        ),
        out_specs=(
            P("gx", ("gy", "gz")),
            P("gx", ("gy", "gz")),
            P("gy", ("gx", "gz")),
            P(("gx", "gz"), "gy"),
        ),
        check_vma=False,
    )
```

```python
import jax
import jax.numpy as jnp
from jax import lax
from jax.experimental import pallas as pl
from jax.experimental.pallas import tpu as pltpu
from jax.sharding import PartitionSpec as P

half_root = 0.7071067811865476
inv_root_tau = 0.3989422804014327
bf16 = jnp.bfloat16
f32 = jnp.float32


def gelu_value(preact):
    return 0.5 * preact * (1.0 + jax.scipy.special.erf(preact * half_root))


def gelu_slope(preact):
    return 0.5 * (
        1.0 + jax.scipy.special.erf(preact * half_root)
    ) + preact * inv_root_tau * jnp.exp(-0.5 * preact * preact)


def dot_nn(left, right):
    return lax.dot_general(left, right, (((1,), (0,)), ((), ())), preferred_element_type=f32)


def dot_tn(left, right):
    return lax.dot_general(left, right, (((0,), (0,)), ((), ())), preferred_element_type=f32)


def dot_nt(left, right):
    return lax.dot_general(left, right, (((1,), (1,)), ((), ())), preferred_element_type=f32)


def corner(place):
    return place ^ (place >> 1)


GY_PAIRS = {
    2: [(g, g ^ 4) for g in range(8)],
    1: [(g, (g & 4) | (3 - (g & 3))) for g in range(8)],
    0: [(g, g ^ 1) for g in range(8)],
}
GZ_PAIRS = {step: [(g, corner(corner(g) ^ step)) for g in range(4)] for step in (1, 2, 3)}
CORE_PAIRS = [(g, g ^ 1) for g in range(4)]
HIGH_PAIRS = [(g, g ^ 2) for g in range(4)]

PARTS = 3
ORDERS = ((2, 1, 0), (1, 0, 2), (0, 2, 1))
SLOT = 256


def over_gy(block, bit):
    return lax.ppermute(block, "gy", GY_PAIRS[bit])


def over_gz(block, step):
    return lax.ppermute(block, "gz", GZ_PAIRS[step])


def over_core(block):
    return lax.ppermute(block, "gx", CORE_PAIRS)


def over_high(block):
    return lax.ppermute(block, "gx", HIGH_PAIRS)


def pick(array, axis, index):
    return lax.index_in_dim(array, index, axis, keepdims=False)


def dyn(array, index):
    return lax.dynamic_index_in_dim(array, index, 0, keepdims=False)


def pass_on(*refs):
    pass


def gate(values, last):
    values, last = tuple(values), tuple(last)
    anywhere = pl.BlockSpec(memory_space=pl.ANY)
    return pl.pallas_call(
        pass_on,
        out_shape=[jax.ShapeDtypeStruct(v.shape, v.dtype) for v in values],
        in_specs=[anywhere] * (len(values) + len(last)),
        out_specs=[anywhere] * len(values),
        input_output_aliases={i: i for i in range(len(values))},
        compiler_params=pltpu.CompilerParams(vmem_limit_bytes=1 << 20),
    )(*values, *last)


def per_device(tokens, weight_in, weight_out, grad_out):
    gy = lax.axis_index("gy")
    gy_id = (gy & 4) | corner(gy & 3)
    gz_id = corner(lax.axis_index("gz"))
    rows = tokens.shape[0] // 8
    width = tokens.shape[1]
    hidden = weight_in.shape[1]
    part = hidden // PARTS
    slot = max(SLOT, width)
    depth = 4 * width

    both = jnp.concatenate([tokens, grad_out], axis=1).reshape(8, rows, 2 * width)
    own = jnp.stack([dyn(both, p ^ gy_id) for p in range(8)])
    far = over_high(own)
    arrived = [[over_gz(half, step) for step in (1, 2, 3)] for half in (own, far)]
    weights = (lambda u: dot_nn(u, weight_in), lambda u: dot_nt(u, weight_out))
    sides, terms = [], []
    for half, got in zip((own, far), arrived):
        if terms:
            got = gate(got, terms[0])
        square = jnp.stack([half, *got])
        square = [dyn(square, corner(p) ^ gz_id) for p in range(4)]
        mine = [jnp.concatenate([s[..., lo : lo + width] for s in square], axis=-1) for lo in (0, width)]
        sides.append([jnp.stack([m, over_core(m)], axis=1).reshape(2, 2, 2, 2 * rows, depth) for m in mine])
        terms.append(
            [
                times(side.reshape(-1, depth)).astype(bf16).reshape(2, 2, 2, 2 * rows, hidden)
                for times, side in zip(weights, sides[-1])
            ]
        )
    features, grad_feats = (jnp.stack([s[i] for s in sides], axis=3) for i in range(2))

    def add(left, right):
        return left.astype(f32) + right.astype(f32)

    spans = [(i * part, (i + 1) * part) for i in range(PARTS)]
    cubes = ([], [])
    for (lo, hi), (first, second, third) in zip(spans, ORDERS):
        axis = 1 + [bit for bit in (2, 1, 0) if bit != first].index(second)
        away, held = (
            jnp.stack([jnp.stack([pick(half[i][..., lo:hi], 2 - first, k) for half in terms], axis=2) for i in range(2)])
            for k in (1, 0)
        )
        held = add(held, over_gy(away, first)).astype(bf16).reshape(2, 2, 2, 4 * rows, part)
        held = add(pick(held, axis, 0), over_gy(pick(held, axis, 1), second)).astype(bf16)
        total = add(held[:, 0], over_gy(held[:, 1], third))
        active = gelu_value(total[0]).astype(bf16)
        grad = (total[1] * gelu_slope(total[0])).astype(bf16)
        piece = jnp.stack([active, grad])
        pair = jnp.stack([piece, over_gy(piece, third)], axis=1)
        square = jnp.stack([pair, over_gy(pair, second)], axis=1)
        if not cubes[0]:
            begun = pair
        axes = [(first, second, third).index(bit) for bit in (2, 1, 0)]
        for side, full in zip(square, cubes):
            cube = jnp.stack([side, over_gy(side, first)])
            full.append(cube.transpose(*axes, 3, 4).reshape(2, 2, 2, 2, 2, rows, part))
    active_rows, grad_rows = (jnp.concatenate(full, axis=-1) for full in cubes)

    gz_late = gz_id + (begun[0, 0, 0, 0].astype(f32) * 0.0).astype(jnp.int32)

    def slots(pieces, axis, fill):
        full = []
        for p in range(4):
            place = corner(p ^ gz_late)
            low = jnp.where(place & 1 == 1, pieces[1], pieces[0])
            high = jnp.where(place & 1 == 1, pieces[3], pieces[2])
            piece = jnp.where(place >= 2, high, low)
            wide = [(0, 0), (0, 0)]
            wide[axis] = fill
            full.append(jnp.pad(piece, wide))
        return jnp.concatenate(full, axis=axis)

    slots_out = slots([weight_out[:, p * width : (p + 1) * width] for p in range(4)], 1, (0, slot - width))
    slots_in = slots([weight_in[p * width : (p + 1) * width] for p in range(4)], 0, (slot - width, 0))

    def core_sum(times, full):
        away = times(full[:, :, :, :, 1].reshape(-1, hidden)).astype(bf16)
        return add(times(full[:, :, :, :, 0].reshape(-1, hidden)), over_core(away)).astype(bf16)

    out_mine = core_sum(lambda u: dot_nn(u, slots_out), active_rows)
    grad_mine = core_sum(lambda u: dot_nt(u, slots_in), grad_rows)
    lap = slot // 2

    def joined(p):
        left, right = (side[:, p * slot : (p + 1) * slot] for side in (out_mine, grad_mine))
        return jnp.concatenate([left[:, :lap], left[:, lap:] + right[:, :lap], right[:, lap:]], axis=1)

    pieces = [joined(p).reshape(8, 2, rows, 3 * lap) for p in range(4)]
    orders = ((1, 2), (2, 1))
    got = [over_gz(jnp.stack([pieces[f][:, h], pieces[3][:, h]]), f) for h, (f, s) in enumerate(orders)]
    features, grad_feats = gate([features, grad_feats], [out_mine, grad_mine])
    grad_weight_out = dot_tn(active_rows.reshape(-1, hidden), grad_feats.reshape(-1, depth)).astype(bf16)
    grad_weight_in = dot_tn(features.reshape(-1, depth), grad_rows.reshape(-1, hidden)).astype(bf16)
    got = gate(got, [grad_weight_out])
    near = [
        add(jnp.stack([pieces[0][:, h], pieces[s][:, h]]), got[h]).astype(bf16) for h, (f, s) in enumerate(orders)
    ]
    got = gate([over_gz(near[h][1], s) for h, (f, s) in enumerate(orders)], [grad_weight_in])
    total = [add(side[0], block) for side, block in zip(near, got)]
    total = add(total[0], over_high(total[1].astype(bf16))).astype(bf16)
    total = jnp.concatenate([dyn(total, p ^ gy_id) for p in range(8)], axis=0)
    return (total[:, :width], total[:, -width:], grad_weight_in, grad_weight_out)


def solution(mesh):
    return jax.shard_map(
        per_device,
        mesh=mesh,
        in_specs=(
            P("gx", ("gy", "gz")),
            P("gy", ("gx", "gz")),
            P(("gx", "gz"), "gy"),
            P("gx", ("gy", "gz")),
        ),
        out_specs=(
            P("gx", ("gy", "gz")),
            P("gx", ("gy", "gz")),
            P("gy", ("gx", "gz")),
            P(("gx", "gz"), "gy"),
        ),
        check_vma=False,
    )
```

```python
import jax
import jax.numpy as jnp
from jax import lax
from jax.experimental import pallas as pl
from jax.experimental.pallas import tpu as pltpu
from jax.sharding import PartitionSpec as P

half_root = 0.7071067811865476
inv_root_tau = 0.3989422804014327
bf16 = jnp.bfloat16
f32 = jnp.float32


def gelu_value(preact):
    return 0.5 * preact * (1.0 + jax.scipy.special.erf(preact * half_root))


def gelu_slope(preact):
    return 0.5 * (
        1.0 + jax.scipy.special.erf(preact * half_root)
    ) + preact * inv_root_tau * jnp.exp(-0.5 * preact * preact)


def dot_nn(left, right):
    return lax.dot_general(left, right, (((1,), (0,)), ((), ())), preferred_element_type=f32)


def dot_tn(left, right):
    return lax.dot_general(left, right, (((0,), (0,)), ((), ())), preferred_element_type=f32)


def dot_nt(left, right):
    return lax.dot_general(left, right, (((1,), (1,)), ((), ())), preferred_element_type=f32)


def corner(place):
    return place ^ (place >> 1)


GY_PAIRS = {
    2: [(g, g ^ 4) for g in range(8)],
    1: [(g, (g & 4) | (3 - (g & 3))) for g in range(8)],
    0: [(g, g ^ 1) for g in range(8)],
}
GZ_PAIRS = {step: [(g, corner(corner(g) ^ step)) for g in range(4)] for step in (1, 2, 3)}
CORE_PAIRS = [(g, g ^ 1) for g in range(4)]
HIGH_PAIRS = [(g, g ^ 2) for g in range(4)]

PARTS = 3
ORDERS = ((1, 0, 2), (0, 2, 1), (2, 1, 0))
SLOT = 256


def over_gy(block, bit):
    return lax.ppermute(block, "gy", GY_PAIRS[bit])


def over_gz(block, step):
    return lax.ppermute(block, "gz", GZ_PAIRS[step])


def over_core(block):
    return lax.ppermute(block, "gx", CORE_PAIRS)


def over_high(block):
    return lax.ppermute(block, "gx", HIGH_PAIRS)


def pick(array, axis, index):
    return lax.index_in_dim(array, index, axis, keepdims=False)


def dyn(array, index):
    return lax.dynamic_index_in_dim(array, index, 0, keepdims=False)


def pass_on(*refs):
    pass


def gate(values, last):
    values, last = tuple(values), tuple(last)
    anywhere = pl.BlockSpec(memory_space=pl.ANY)
    return pl.pallas_call(
        pass_on,
        out_shape=[jax.ShapeDtypeStruct(v.shape, v.dtype) for v in values],
        in_specs=[anywhere] * (len(values) + len(last)),
        out_specs=[anywhere] * len(values),
        input_output_aliases={i: i for i in range(len(values))},
        compiler_params=pltpu.CompilerParams(vmem_limit_bytes=1 << 20),
    )(*values, *last)


def per_device(tokens, weight_in, weight_out, grad_out):
    gy = lax.axis_index("gy")
    gy_id = (gy & 4) | corner(gy & 3)
    gz_id = corner(lax.axis_index("gz"))
    rows = tokens.shape[0] // 8
    width = tokens.shape[1]
    hidden = weight_in.shape[1]
    part = hidden // PARTS
    slot = max(SLOT, width)
    depth = 4 * width

    both = jnp.concatenate([tokens, grad_out], axis=1).reshape(8, rows, 2 * width)
    own = jnp.stack([dyn(both, p ^ gy_id) for p in range(8)])
    far = over_high(own)
    arrived = [[over_gz(half, step) for step in (1, 2, 3)] for half in (own, far)]
    weights = (lambda u: dot_nn(u, weight_in), lambda u: dot_nt(u, weight_out))
    sides, terms = [], []
    for half, got in zip((own, far), arrived):
        if terms:
            got = gate(got, terms[0])
        square = jnp.stack([half, *got])
        square = [dyn(square, corner(p) ^ gz_id) for p in range(4)]
        mine = [jnp.concatenate([s[..., lo : lo + width] for s in square], axis=-1) for lo in (0, width)]
        sides.append([jnp.stack([m, over_core(m)], axis=1).reshape(2, 2, 2, 2 * rows, depth) for m in mine])
        terms.append(
            [
                times(side.reshape(-1, depth)).astype(bf16).reshape(2, 2, 2, 2 * rows, hidden)
                for times, side in zip(weights, sides[-1])
            ]
        )
    features, grad_feats = (jnp.stack([s[i] for s in sides], axis=3) for i in range(2))

    def add(left, right):
        return left.astype(f32) + right.astype(f32)

    spans = [(i * part, (i + 1) * part) for i in range(PARTS)]
    cubes = ([], [])
    for (lo, hi), (first, second, third) in zip(spans, ORDERS):
        axis = 1 + [bit for bit in (2, 1, 0) if bit != first].index(second)
        away, held = (
            jnp.stack([jnp.stack([pick(half[i][..., lo:hi], 2 - first, k) for half in terms], axis=2) for i in range(2)])
            for k in (1, 0)
        )
        held = add(held, over_gy(away, first)).astype(bf16).reshape(2, 2, 2, 4 * rows, part)
        held = add(pick(held, axis, 0), over_gy(pick(held, axis, 1), second)).astype(bf16)
        total = add(held[:, 0], over_gy(held[:, 1], third))
        active = gelu_value(total[0]).astype(bf16)
        grad = (total[1] * gelu_slope(total[0])).astype(bf16)
        piece = jnp.stack([active, grad])
        pair = jnp.stack([piece, over_gy(piece, third)], axis=1)
        square = jnp.stack([pair, over_gy(pair, second)], axis=1)
        if not cubes[0]:
            begun = pair
        axes = [(first, second, third).index(bit) for bit in (2, 1, 0)]
        for side, full in zip(square, cubes):
            cube = jnp.stack([side, over_gy(side, first)])
            full.append(cube.transpose(*axes, 3, 4).reshape(2, 2, 2, 2, 2, rows, part))
    active_rows, grad_rows = (jnp.concatenate(full, axis=-1) for full in cubes)

    gz_late = gz_id + (begun[0, 0, 0, 0].astype(f32) * 0.0).astype(jnp.int32)

    def slots(pieces, axis, fill):
        full = []
        for p in range(4):
            place = corner(p ^ gz_late)
            low = jnp.where(place & 1 == 1, pieces[1], pieces[0])
            high = jnp.where(place & 1 == 1, pieces[3], pieces[2])
            piece = jnp.where(place >= 2, high, low)
            wide = [(0, 0), (0, 0)]
            wide[axis] = fill
            full.append(jnp.pad(piece, wide))
        return jnp.concatenate(full, axis=axis)

    slots_out = slots([weight_out[:, p * width : (p + 1) * width] for p in range(4)], 1, (0, slot - width))
    slots_in = slots([weight_in[p * width : (p + 1) * width] for p in range(4)], 0, (slot - width, 0))

    def core_sum(times, full):
        away = times(full[:, :, :, :, 1].reshape(-1, hidden)).astype(bf16)
        return add(times(full[:, :, :, :, 0].reshape(-1, hidden)), over_core(away)).astype(bf16)

    out_mine = core_sum(lambda u: dot_nn(u, slots_out), active_rows)
    grad_mine = core_sum(lambda u: dot_nt(u, slots_in), grad_rows)
    lap = slot // 2

    def joined(p):
        left, right = (side[:, p * slot : (p + 1) * slot] for side in (out_mine, grad_mine))
        return jnp.concatenate([left[:, :lap], left[:, lap:] + right[:, :lap], right[:, lap:]], axis=1)

    pieces = [joined(p).reshape(8, 2, rows, 3 * lap) for p in range(4)]
    orders = ((1, 2), (2, 1))
    got = [over_gz(jnp.stack([pieces[f][:, h], pieces[3][:, h]]), f) for h, (f, s) in enumerate(orders)]
    features, grad_feats = gate([features, grad_feats], [out_mine, grad_mine])
    grad_weight_out = dot_tn(active_rows.reshape(-1, hidden), grad_feats.reshape(-1, depth)).astype(bf16)
    grad_weight_in = dot_tn(features.reshape(-1, depth), grad_rows.reshape(-1, hidden)).astype(bf16)
    got = gate(got, [grad_weight_out])
    near = [
        add(jnp.stack([pieces[0][:, h], pieces[s][:, h]]), got[h]).astype(bf16) for h, (f, s) in enumerate(orders)
    ]
    got = gate([over_gz(near[h][1], s) for h, (f, s) in enumerate(orders)], [grad_weight_in])
    total = [add(side[0], block) for side, block in zip(near, got)]
    total = add(total[0], over_high(total[1].astype(bf16))).astype(bf16)
    total = jnp.concatenate([dyn(total, p ^ gy_id) for p in range(8)], axis=0)
    return (total[:, :width], total[:, -width:], grad_weight_in, grad_weight_out)


def solution(mesh):
    return jax.shard_map(
        per_device,
        mesh=mesh,
        in_specs=(
            P("gx", ("gy", "gz")),
            P("gy", ("gx", "gz")),
            P(("gx", "gz"), "gy"),
            P("gx", ("gy", "gz")),
        ),
        out_specs=(
            P("gx", ("gy", "gz")),
            P("gx", ("gy", "gz")),
            P("gy", ("gx", "gz")),
            P(("gx", "gz"), "gy"),
        ),
        check_vma=False,
    )
```
